1024 devices in a mesh: replica: 4 (over y_hi, core), fsdp: 256 (over y_lo, z, x).
Axes of the slice: x: 4, y: 8 (y_hi: 2, y_lo: 4; y = y_hi * 4 + y_lo), z: 16, core: 2. Of those that a mesh axis runs over, the one named last changes fastest.
Arguments:
- tokens: bfloat16 [4, 49152, 4096], P('replica', 'fsdp'), may hold values from -6 to 6
- gain: float32 [4, 4096], P('replica'), may hold values from 0.5 to 1.5
- key_cotangent: bfloat16 [4, 49152, 512], P('replica', 'fsdp'), may hold values from -6 to 6
- global_params: float32 [4096, 512], P('fsdp'), may hold values from -0.09375 to 0.09375
- local_params: bfloat16 [4, 4096, 512], P('replica', 'fsdp'), may hold values from -0.09375 to 0.09375
- momentum: float32 [4096, 512], P('fsdp'), may hold values from -0.06 to 0.06
- sign_bits: int32 [512], replicated, may hold values from 0 to 1
Outputs:
- key_out: bfloat16 [4, 49152, 512], P('replica', 'fsdp')
- grad_tokens: bfloat16 [4, 49152, 4096], P('replica', 'fsdp')
- new_params: float32 [4096, 512], P('fsdp')
- new_momentum: float32 [4096, 512], P('fsdp')
The draws below stay inside these ranges and needn't reach their ends.
All inputs are finite; a program needn't handle non-finite values. Where the reference program divides by a largest or mean magnitude, that divisor is 1e-20 or more.
Results may differ from the reference program's by a relative error of at most 0.023.
Values may be sent and summed in bfloat16 or wider, within the bound.
No kernel may reach another device: no remote copies, remote signals or barrier semaphores. Data moves between devices by JAX's collectives and lax.ppermute only.
A program may use at most 32 MiB of HBM per device.

```python
import math
import jax
import jax.numpy as jnp
import numpy as np
from jax import lax

D = 4096
KW = 512
HB = 128
TOK_DEV = 192
TOKENS = 49152
N_REPLICA = 4
N_FSDP = 256


def plant(values, stream_key, smallest, high):
    longest = values.shape.index(max(values.shape))
    spots = []
    for shift in (0, 1):
        where = [jax.random.randint(jax.random.fold_in(stream_key, axis), (), 0, length) for axis, length in enumerate(values.shape)]
        where[longest] = (where[longest] + shift) % values.shape[longest]
        spots.append(tuple(where))
    return values.at[spots[0]].set(smallest).at[spots[1]].set(high)


def level_of(key, shape, shards, smallest, high):
    loudness = 1.0
    for axis_at, shards_of in shards:
        heights = jax.random.uniform(jax.random.fold_in(jax.random.fold_in(key, 6), axis_at), (shards_of,), jnp.float32, smallest / len(shards), high / len(shards))
        loudness = loudness * jnp.repeat(jnp.exp(heights), shape[axis_at] // shards_of).reshape((-1,) + (1,) * (len(shape) - 1 - axis_at))
    return loudness


def normal_values(stream_key, extent, spread, most, shards=(), kind=jnp.bfloat16):
    values = jax.random.normal(stream_key, extent, jnp.float32) * spread
    if len(shards) > 0:
        values = level_of(stream_key, extent, shards, -0.22, 0.18) * values
    return jnp.clip(values, min=-most, max=most).astype(kind)


def setup_inputs(seed: int = 0) -> dict:
    arg_keys = jax.random.split(jax.random.key(seed), 8)
    tokens = normal_values(arg_keys[0], (N_REPLICA, TOKENS, D), 1.0, 6.0, ((0, 4), (1, 256)))
    gain = jnp.clip(1.0 + 0.1 * jax.random.normal(arg_keys[1], (N_REPLICA, D), jnp.float32), 0.5, 1.5)
    key_cotangent = normal_values(arg_keys[2], (N_REPLICA, TOKENS, KW), 1.0, 6.0, ((0, 4), (1, 256)))
    global_params = normal_values(arg_keys[3], (D, KW), D ** -0.5, 0.09375, ((0, 256),), jnp.float32)
    local_params = normal_values(arg_keys[4], (N_REPLICA, D, KW), D ** -0.5, 0.09375, ((0, 4), (1, 256)))
    momentum = normal_values(arg_keys[5], (D, KW), 0.01, 0.06, ((0, 256),), jnp.float32)
    sign_bits = plant(jax.random.randint(arg_keys[6], (KW,), 0, 2), jax.random.fold_in(arg_keys[6], 1), 0, 1).astype(jnp.int32)
    return {"tokens": tokens, "gain": gain, "key_cotangent": key_cotangent, "global_params": global_params, "local_params": local_params, "momentum": momentum, "sign_bits": sign_bits}


NORM_EPS = 1e-06
OUTER_MU = 0.9
OUTER_LR = 0.7
CLIP_LEVEL = 2.0

def hadamard(order):
    counter = np.arange(order)
    common = counter[:, None] & counter[None, :]
    parity = common & 0
    shift = 0
    while 1 << shift < order:
        parity = parity ^ common >> shift & 1
        shift = shift + 1
    return jnp.asarray((1 - 2 * parity) / math.sqrt(order), dtype=jnp.float32)

def rotate(values, sign_vec):
    width = values.shape[-1]
    blocks = (values * sign_vec).reshape(values.shape[:-1] + (width // HB, HB))
    return jnp.einsum('...bi,ij->...bj', blocks, hadamard(HB), precision=lax.Precision.HIGHEST)

def clip_terms(rotated):
    block_scale = lax.optimization_barrier(jnp.mean(jnp.abs(rotated), axis=-1, keepdims=True)) + NORM_EPS
    return jnp.clip(rotated / block_scale, -CLIP_LEVEL, CLIP_LEVEL) * block_scale

def outer_update(global_rows, moment_rows, averaged, sign_vec):
    row_count, width = global_rows.shape
    blocks = averaged.reshape(row_count, width // HB, HB)
    restored = jnp.einsum('rbi,ij->rbj', blocks, hadamard(HB), precision=lax.Precision.HIGHEST)
    pseudo = restored.reshape(row_count, width) * sign_vec
    fresh_moment = OUTER_MU * moment_rows + pseudo
    fresh_params = global_rows - OUTER_LR * (pseudo + OUTER_MU * fresh_moment)
    return (fresh_params, fresh_moment)

def layer_pass(tok_rows, gain_vec, weight, cotangent):
    tok_float = tok_rows.astype(jnp.float32)
    inverse = lax.rsqrt(lax.optimization_barrier(jnp.mean(tok_float * tok_float, axis=-1, keepdims=True)) + NORM_EPS)
    normed = tok_float * inverse
    hidden = (normed * gain_vec).astype(jnp.bfloat16)
    keys = jnp.dot(hidden, weight, preferred_element_type=jnp.float32).astype(jnp.bfloat16)
    back = jnp.dot(cotangent, weight.T, preferred_element_type=jnp.float32)
    scaled = back * gain_vec
    centre = lax.optimization_barrier(jnp.mean(scaled * normed, axis=-1, keepdims=True))
    grads = (inverse * (scaled - normed * centre)).astype(jnp.bfloat16)
    return (keys, grads)

def reference(tokens, gain, key_cotangent, global_params, local_params, momentum, sign_bits):
    sign_vec = (2 * sign_bits - 1).astype(jnp.float32)
    drift = global_params[None] - local_params.astype(jnp.float32)
    terms = clip_terms(rotate(drift, sign_vec)).astype(jnp.bfloat16)
    terms = lax.optimization_barrier(terms)
    averaged = lax.optimization_barrier(jnp.sum(terms.astype(jnp.float32), axis=0)).reshape(D, KW) / N_REPLICA
    new_params, new_momentum = outer_update(global_params, momentum, averaged, sign_vec)
    weight = new_params.astype(jnp.bfloat16)
    tok_blocks = tokens.reshape(N_REPLICA * N_FSDP, TOK_DEV, D)
    cot_blocks = key_cotangent.reshape(N_REPLICA * N_FSDP, TOK_DEV, KW)
    owners = jnp.arange(N_REPLICA * N_FSDP, dtype=jnp.int32) // N_FSDP

    def one_block(operands):
        block_tok, block_cot, owner = operands
        return layer_pass(block_tok, gain[owner], weight, block_cot)
    key_blocks, grad_blocks = lax.map(one_block, (tok_blocks, cot_blocks, owners))
    key_out = key_blocks.reshape(N_REPLICA, TOKENS, KW)
    grad_tokens = grad_blocks.reshape(N_REPLICA, TOKENS, D)
    return (key_out, grad_tokens, new_params, new_momentum)
```

```python
import math

import jax
import jax.numpy as jnp
import numpy as np
from jax import lax
from jax.sharding import Mesh, PartitionSpec as P

HB = 128


NORM_EPS = 1e-06
OUTER_MU = 0.9
OUTER_LR = 0.7
CLIP_LEVEL = 2.0

REPLICA = ("yh", "core")
FSDP = ("yl", "zh", "zl", "x")
SIZES = {"yh": 2, "core": 2, "yl": 4, "zh": 4, "zl": 4, "x": 4}


def hadamard(order):
    counter = np.arange(order)
    common = counter[:, None] & counter[None, :]
    parity = common & 0
    shift = 0
    while 1 << shift < order:
        parity = parity ^ common >> shift & 1
        shift = shift + 1
    return jnp.asarray((1 - 2 * parity) / math.sqrt(order), dtype=jnp.float32)


def rotate(values, sign_vec):
    width = values.shape[-1]
    blocks = (values * sign_vec).reshape(values.shape[:-1] + (width // HB, HB))
    return jnp.einsum("...bi,ij->...bj", blocks, hadamard(HB), precision=lax.Precision.HIGHEST)


def clip_terms(rotated):
    block_scale = jnp.mean(jnp.abs(rotated), axis=-1, keepdims=True) + NORM_EPS
    return jnp.clip(rotated / block_scale, -CLIP_LEVEL, CLIP_LEVEL) * block_scale


def outer_update(global_rows, moment_rows, averaged, sign_vec):
    row_count, width = global_rows.shape
    blocks = averaged.reshape(row_count, width // HB, HB)
    restored = jnp.einsum("rbi,ij->rbj", blocks, hadamard(HB), precision=lax.Precision.HIGHEST)
    pseudo = restored.reshape(row_count, width) * sign_vec
    fresh_moment = OUTER_MU * moment_rows + pseudo
    fresh_params = global_rows - OUTER_LR * (pseudo + OUTER_MU * fresh_moment)
    return (fresh_params, fresh_moment)


def gather(block, axes):
    count = math.prod(SIZES[axis] for axis in axes)
    copies = jnp.broadcast_to(block[None], (count,) + block.shape)
    return lax.all_to_all(copies, axes, 0, 0, tiled=True)


def body(tokens, gain, key_cotangent, global_params, local_params, momentum, sign_bits):
    sign_vec = (2 * sign_bits - 1).astype(jnp.float32)
    drift = global_params - local_params[0].astype(jnp.float32)
    row_count, width = drift.shape
    terms = clip_terms(rotate(drift, sign_vec)).reshape(row_count, width).astype(jnp.bfloat16)
    all_terms = gather(terms, REPLICA)
    replicas = all_terms.shape[0]
    summed = jnp.sum(all_terms.astype(jnp.float32), axis=0)
    new_params, new_momentum = outer_update(global_params, momentum, summed / replicas, sign_vec)
    weight_part = new_params.astype(jnp.bfloat16)

    half = width // 2
    core = lax.axis_index("core")
    mine = jnp.where(core == 0, weight_part[:, :half], weight_part[:, half:])
    got = gather(mine, ("zh",))
    got = gather(got, ("yl", "zl"))
    got = gather(got, ("x",))
    got = got.reshape(4, 4, 4, 4, row_count, half).transpose(1, 3, 2, 0, 4, 5)
    got = got.reshape(-1, half)
    other = lax.ppermute(got, "core", [(0, 1), (1, 0)])
    low = jnp.where(core == 0, got, other)
    high = jnp.where(core == 0, other, got)
    weight = jnp.concatenate([low, high], axis=1)

    tok_float = tokens[0].astype(jnp.float32)
    gain_vec = gain[0]
    cotangent = key_cotangent[0]
    inverse = lax.rsqrt(jnp.mean(tok_float * tok_float, axis=-1, keepdims=True) + NORM_EPS)
    normed = tok_float * inverse
    hidden = (normed * gain_vec).astype(jnp.bfloat16)
    keys = jnp.dot(hidden, weight, preferred_element_type=jnp.float32)
    back = lax.dot_general(cotangent, weight, (((1,), (1,)), ((), ())), preferred_element_type=jnp.float32)
    scaled = back * gain_vec
    centre = jnp.mean(scaled * normed, axis=-1, keepdims=True)
    grads = (inverse * (scaled - normed * centre)).astype(jnp.bfloat16)
    key_out = keys.astype(jnp.bfloat16)[None]
    grad_tokens = grads[None]
    return (key_out, grad_tokens, new_params, new_momentum)


def solution(mesh):
    fine = Mesh(mesh.devices.reshape(tuple(SIZES.values())), tuple(SIZES))
    in_specs = (
        P(REPLICA, FSDP, None),
        P(REPLICA, None),
        P(REPLICA, FSDP, None),
        P(FSDP, None),
        P(REPLICA, FSDP, None),
        P(FSDP, None),
        P(),
    )
    out_specs = (
        P(REPLICA, FSDP, None),
        P(REPLICA, FSDP, None),
        P(FSDP, None),
        P(FSDP, None),
    )
    return jax.shard_map(body, mesh=fine, in_specs=in_specs, out_specs=out_specs, check_vma=False)
```

```python
import math

import jax
import jax.numpy as jnp
import numpy as np
from jax import lax
from jax.sharding import Mesh, PartitionSpec as P

HB = 128


NORM_EPS = 1e-06
OUTER_MU = 0.9
OUTER_LR = 0.7
CLIP_LEVEL = 2.0

REPLICA = ("yh", "core")
FSDP = ("y1", "y0", "zh", "z0", "x")
SIZES = {"yh": 2, "core": 2, "y1": 2, "y0": 2, "zh": 8, "z0": 2, "x": 4}


def hadamard(order):
    counter = np.arange(order)
    common = counter[:, None] & counter[None, :]
    parity = common & 0
    shift = 0
    while 1 << shift < order:
        parity = parity ^ common >> shift & 1
        shift = shift + 1
    return jnp.asarray((1 - 2 * parity) / math.sqrt(order), dtype=jnp.float32)


def rotate(values, sign_vec):
    width = values.shape[-1]
    blocks = (values * sign_vec).reshape(values.shape[:-1] + (width // HB, HB))
    return jnp.einsum("...bi,ij->...bj", blocks, hadamard(HB), precision=lax.Precision.HIGHEST)


def clip_terms(rotated):
    block_scale = jnp.mean(jnp.abs(rotated), axis=-1, keepdims=True) + NORM_EPS
    return jnp.clip(rotated / block_scale, -CLIP_LEVEL, CLIP_LEVEL) * block_scale


def outer_update(global_rows, moment_rows, averaged, sign_vec):
    row_count, width = global_rows.shape
    blocks = averaged.reshape(row_count, width // HB, HB)
    restored = jnp.einsum("rbi,ij->rbj", blocks, hadamard(HB), precision=lax.Precision.HIGHEST)
    pseudo = restored.reshape(row_count, width) * sign_vec
    fresh_moment = OUTER_MU * moment_rows + pseudo
    fresh_params = global_rows - OUTER_LR * (pseudo + OUTER_MU * fresh_moment)
    return (fresh_params, fresh_moment)


def gather(block, axes):
    count = math.prod(SIZES[axis] for axis in axes)
    copies = jnp.broadcast_to(block[None], (count,) + block.shape)
    return lax.all_to_all(copies, axes, 0, 0, tiled=True)


def body(tokens, gain, key_cotangent, global_params, local_params, momentum, sign_bits):
    sign_vec = (2 * sign_bits - 1).astype(jnp.float32)
    drift = global_params - local_params[0].astype(jnp.float32)
    row_count, width = drift.shape
    terms = clip_terms(rotate(drift, sign_vec)).reshape(row_count, width).astype(jnp.bfloat16)
    all_terms = gather(terms, REPLICA)
    replicas = all_terms.shape[0]
    summed = jnp.sum(all_terms.astype(jnp.float32), axis=0)
    new_params, new_momentum = outer_update(global_params, momentum, summed / replicas, sign_vec)
    weight_part = new_params.astype(jnp.bfloat16)

    half = width // 2
    core = lax.axis_index("core")
    mine = jnp.where(core == 0, weight_part[:, :half], weight_part[:, half:])
    got = gather(mine, ("y1", "zh"))
    got = gather(got, ("y0", "z0", "x"))
    got = got.reshape(2, 2, 4, 2, 8, row_count, half).transpose(3, 0, 4, 1, 2, 5, 6)
    got = got.reshape(-1, half)
    other = lax.ppermute(got, "core", [(0, 1), (1, 0)])
    low = jnp.where(core == 0, got, other)
    high = jnp.where(core == 0, other, got)
    weight = jnp.concatenate([low, high], axis=1)

    tok_float = tokens[0].astype(jnp.float32)
    gain_vec = gain[0]
    cotangent = key_cotangent[0]
    inverse = lax.rsqrt(jnp.mean(tok_float * tok_float, axis=-1, keepdims=True) + NORM_EPS)
    normed = tok_float * inverse
    hidden = (normed * gain_vec).astype(jnp.bfloat16)
    keys = jnp.dot(hidden, weight, preferred_element_type=jnp.float32)
    back = lax.dot_general(cotangent, weight, (((1,), (1,)), ((), ())), preferred_element_type=jnp.float32)
    scaled = back * gain_vec
    centre = jnp.mean(scaled * normed, axis=-1, keepdims=True)
    grads = (inverse * (scaled - normed * centre)).astype(jnp.bfloat16)
    key_out = keys.astype(jnp.bfloat16)[None]
    grad_tokens = grads[None]
    return (key_out, grad_tokens, new_params, new_momentum)


def solution(mesh):
    fine = Mesh(mesh.devices.reshape(tuple(SIZES.values())), tuple(SIZES))
    in_specs = (
        P(REPLICA, FSDP, None),
        P(REPLICA, None),
        P(REPLICA, FSDP, None),
        P(FSDP, None),
        P(REPLICA, FSDP, None),
        P(FSDP, None),
        P(),
    )
    out_specs = (
        P(REPLICA, FSDP, None),
        P(REPLICA, FSDP, None),
        P(FSDP, None),
        P(FSDP, None),
    )
    return jax.shard_map(body, mesh=fine, in_specs=in_specs, out_specs=out_specs, check_vma=False)
```

```python
import math

import jax
import jax.numpy as jnp
import numpy as np
from jax import lax
from jax.sharding import Mesh, PartitionSpec as P

HB = 128


NORM_EPS = 1e-06
OUTER_MU = 0.9
OUTER_LR = 0.7
CLIP_LEVEL = 2.0

REPLICA = ("yh", "core")
FSDP = ("y1", "y0", "zh", "z0", "x1", "x0")
SIZES = {"yh": 2, "core": 2, "y1": 2, "y0": 2, "zh": 8, "z0": 2, "x1": 2, "x0": 2}
AXES = tuple(SIZES)


def hadamard(order):
    counter = np.arange(order)
    common = counter[:, None] & counter[None, :]
    parity = common & 0
    shift = 0
    while 1 << shift < order:
        parity = parity ^ common >> shift & 1
        shift = shift + 1
    return jnp.asarray((1 - 2 * parity) / math.sqrt(order), dtype=jnp.float32)


def rotate(values, sign_vec):
    width = values.shape[-1]
    blocks = (values * sign_vec).reshape(values.shape[:-1] + (width // HB, HB))
    return jnp.einsum("...bi,ij->...bj", blocks, hadamard(HB), precision=lax.Precision.HIGHEST)


def clip_terms(rotated):
    block_scale = jnp.mean(jnp.abs(rotated), axis=-1, keepdims=True) + NORM_EPS
    return jnp.clip(rotated / block_scale, -CLIP_LEVEL, CLIP_LEVEL) * block_scale


def outer_update(global_rows, moment_rows, averaged, sign_vec):
    row_count, width = global_rows.shape
    blocks = averaged.reshape(row_count, width // HB, HB)
    restored = jnp.einsum("rbi,ij->rbj", blocks, hadamard(HB), precision=lax.Precision.HIGHEST)
    pseudo = restored.reshape(row_count, width) * sign_vec
    fresh_moment = OUTER_MU * moment_rows + pseudo
    fresh_params = global_rows - OUTER_LR * (pseudo + OUTER_MU * fresh_moment)
    return (fresh_params, fresh_moment)


def cubes():
    groups = []
    for core in range(2):
        for y in range(0, 8, 2):
            for z in range(0, 16, 2):
                for x in range(0, 4, 2):
                    group = []
                    for odd in np.ndindex(2, 2, 2):
                        step = [bit * (1 - 2 * core) for bit in odd]
                        y_at, z_at, x_at = (y + step[0]) % 8, (z + step[1]) % 16, (x + step[2]) % 4
                        group.append((((y_at // 4 * 2 + core) * 4 + y_at % 4) * 16 + z_at) * 4 + x_at)
                    groups.append(group)
    return groups


def gather(block, axes, count, groups=None):
    copies = jnp.broadcast_to(block[None], (count,) + block.shape)
    return lax.all_to_all(copies, axes, 0, 0, axis_index_groups=groups, tiled=True)


def body(tokens, gain, key_cotangent, global_params, local_params, momentum, sign_bits):
    sign_vec = (2 * sign_bits - 1).astype(jnp.float32)
    all_local = gather(local_params[0], REPLICA, 4)
    drift = global_params[None] - all_local.astype(jnp.float32)
    replicas, row_count, width = drift.shape
    terms = clip_terms(rotate(drift, sign_vec)).reshape(replicas, row_count, width).astype(jnp.bfloat16)
    summed = jnp.sum(terms.astype(jnp.float32), axis=0)
    new_params, new_momentum = outer_update(global_params, momentum, summed / replicas, sign_vec)
    weight_part = new_params.astype(jnp.bfloat16)

    half = width // 2
    core = lax.axis_index("core")
    mine = jnp.where(core == 0, weight_part[:, :half], weight_part[:, half:])
    got = gather(mine, ("y1", "zh", "x1"), 32)
    got = gather(got, AXES, 8, cubes())
    got = got.reshape(2, 2, 2, 2, 8, 2, row_count, half).transpose(3, 0, 4, 1, 5, 2, 6, 7)
    got = got.reshape(-1, half)
    other = lax.ppermute(got, "core", [(0, 1), (1, 0)])

    tok_float = tokens[0].astype(jnp.float32)
    gain_vec = gain[0]
    inverse = lax.rsqrt(jnp.mean(tok_float * tok_float, axis=-1, keepdims=True) + NORM_EPS)
    normed = tok_float * inverse
    hidden = (normed * gain_vec).astype(jnp.bfloat16)
    low, high = key_cotangent[0][:, :half], key_cotangent[0][:, half:]

    def both(cotangent, weight):
        keys = jnp.dot(hidden, weight, preferred_element_type=jnp.float32)
        back = lax.dot_general(cotangent, weight, (((1,), (1,)), ((), ())), preferred_element_type=jnp.float32)
        return keys.astype(jnp.bfloat16), back

    keys_mine, back_mine = both(jnp.where(core == 0, low, high), got)
    keys_other, back_other = both(jnp.where(core == 0, high, low), other)
    key_low = jnp.where(core == 0, keys_mine, keys_other)
    key_high = jnp.where(core == 0, keys_other, keys_mine)
    keys = jnp.concatenate([key_low, key_high], axis=1)
    scaled = (back_mine + back_other) * gain_vec
    centre = jnp.mean(scaled * normed, axis=-1, keepdims=True)
    grads = (inverse * (scaled - normed * centre)).astype(jnp.bfloat16)
    return (keys[None], grads[None], new_params, new_momentum)


def solution(mesh):
    fine = Mesh(mesh.devices.reshape(tuple(SIZES.values())), tuple(SIZES))
    in_specs = (
        P(REPLICA, FSDP, None),
        P(REPLICA, None),
        P(REPLICA, FSDP, None),
        P(FSDP, None),
        P(REPLICA, FSDP, None),
        P(FSDP, None),
        P(),
    )
    out_specs = (
        P(REPLICA, FSDP, None),
        P(REPLICA, FSDP, None),
        P(FSDP, None),
        P(FSDP, None),
    )
    return jax.shard_map(body, mesh=fine, in_specs=in_specs, out_specs=out_specs, check_vma=False)
```

```python
import math

import jax
import jax.numpy as jnp
import numpy as np
from jax import lax
from jax.experimental import pallas as pl
from jax.experimental.pallas import tpu as pltpu
from jax.sharding import Mesh, PartitionSpec as P

HB = 128


NORM_EPS = 1e-06
OUTER_MU = 0.9
OUTER_LR = 0.7
CLIP_LEVEL = 2.0

REPLICA = ("yh", "core")
FSDP = ("y1", "y0", "zh", "z0", "x1", "x0")
SIZES = {"yh": 2, "core": 2, "y1": 2, "y0": 2, "zh": 8, "z0": 2, "x1": 2, "x0": 2}
AXES = tuple(SIZES)


def signs():
    common = lax.broadcasted_iota(jnp.int32, (HB, HB), 0) & lax.broadcasted_iota(jnp.int32, (HB, HB), 1)
    for shift in (4, 2, 1):
        common = common ^ (common >> shift)
    return (1 - 2 * (common & 1)).astype(jnp.float32).astype(jnp.bfloat16)


def rotate(values, matrix):
    total = None
    rest = values
    for _ in range(3):
        part = rest.astype(jnp.bfloat16)
        rest = rest - part.astype(jnp.float32)
        product = jnp.dot(part, matrix, preferred_element_type=jnp.float32)
        total = product if total is None else total + product
    return total * (1.0 / math.sqrt(HB))


def update_kernel(local_ref, global_ref, moment_ref, bits_ref, weight_ref, params_ref, fresh_ref):
    replicas, row_count, width = local_ref.shape
    count = width // HB
    matrix = signs()
    sign_vec = (2 * bits_ref[...] - 1).astype(jnp.float32)
    global_rows = global_ref[...]
    pieces = []
    for replica in range(replicas):
        drift = (global_rows - local_ref[replica].astype(jnp.float32)) * sign_vec
        pieces += [drift[:, at * HB : (at + 1) * HB] for at in range(count)]
    rotated = rotate(jnp.concatenate(pieces, axis=0), matrix)
    block_scale = jnp.mean(jnp.abs(rotated), axis=-1, keepdims=True) + NORM_EPS
    terms = jnp.clip(rotated / block_scale, -CLIP_LEVEL, CLIP_LEVEL) * block_scale
    terms = terms.astype(jnp.bfloat16).astype(jnp.float32)
    rows = count * row_count
    summed = terms[:rows]
    for replica in range(1, replicas):
        summed = summed + terms[replica * rows : (replica + 1) * rows]
    restored = rotate(summed / replicas, matrix)
    restored = jnp.concatenate([restored[at * row_count : (at + 1) * row_count] for at in range(count)], axis=1)
    pseudo = restored * sign_vec
    fresh = OUTER_MU * moment_ref[...] + pseudo
    params = global_rows - OUTER_LR * (pseudo + OUTER_MU * fresh)
    fresh_ref[...] = fresh
    params_ref[...] = params
    weight_ref[...] = params.astype(jnp.bfloat16)


def outer_update(all_local, global_params, momentum, sign_bits):
    row_count, width = global_params.shape
    return pl.pallas_call(
        update_kernel,
        out_shape=(
            jax.ShapeDtypeStruct((row_count, width), jnp.bfloat16),
            jax.ShapeDtypeStruct((row_count, width), jnp.float32),
            jax.ShapeDtypeStruct((row_count, width), jnp.float32),
        ),
        in_specs=[pl.BlockSpec(memory_space=pltpu.VMEM)] * 4,
        out_specs=[pl.BlockSpec(memory_space=pltpu.VMEM)] * 3,
        cost_estimate=pl.CostEstimate(flops=20_000_000, bytes_accessed=250_000, transcendentals=0),
    )(all_local, global_params, momentum, sign_bits.reshape(1, width))


def cubes():
    groups = []
    for core in range(2):
        for y in range(0, 8, 2):
            for z in range(0, 16, 2):
                for x in range(0, 4, 2):
                    group = []
                    for odd in np.ndindex(2, 2, 2):
                        step = [bit * (1 - 2 * core) for bit in odd]
                        y_at, z_at, x_at = (y + step[0]) % 8, (z + step[1]) % 16, (x + step[2]) % 4
                        group.append((((y_at // 4 * 2 + core) * 4 + y_at % 4) * 16 + z_at) * 4 + x_at)
                    groups.append(group)
    return groups


def gather(block, axes, count, groups=None):
    copies = jnp.broadcast_to(block[None], (count,) + block.shape)
    return lax.all_to_all(copies, axes, 0, 0, axis_index_groups=groups, tiled=True)


def body(tokens, gain, key_cotangent, global_params, local_params, momentum, sign_bits):
    all_local = gather(local_params[0], REPLICA, 4)
    weight_part, new_params, new_momentum = outer_update(all_local, global_params, momentum, sign_bits)
    row_count, width = global_params.shape

    half = width // 2
    core = lax.axis_index("core")
    mine = jnp.where(core == 0, weight_part[:, :half], weight_part[:, half:])
    got = gather(mine, ("zh",), 8)
    got = gather(got, ("y1", "x1"), 4)
    got = gather(got, AXES, 8, cubes())
    got = got.reshape(2, 2, 2, 2, 2, 8, row_count, half).transpose(3, 0, 5, 1, 4, 2, 6, 7)
    got = got.reshape(-1, half)
    other = lax.ppermute(got, "core", [(0, 1), (1, 0)])

    tok_float = tokens[0].astype(jnp.float32)
    gain_vec = gain[0]
    inverse = lax.rsqrt(jnp.mean(tok_float * tok_float, axis=-1, keepdims=True) + NORM_EPS)
    normed = tok_float * inverse
    hidden = (normed * gain_vec).astype(jnp.bfloat16)
    low, high = key_cotangent[0][:, :half], key_cotangent[0][:, half:]

    def both(cotangent, weight):
        keys = jnp.dot(hidden, weight, preferred_element_type=jnp.float32)
        back = lax.dot_general(cotangent, weight, (((1,), (1,)), ((), ())), preferred_element_type=jnp.float32)
        return keys.astype(jnp.bfloat16), back

    keys_mine, back_mine = both(jnp.where(core == 0, low, high), got)
    keys_other, back_other = both(jnp.where(core == 0, high, low), other)
    keys = jnp.zeros((keys_mine.shape[0], width), jnp.bfloat16)
    keys = lax.dynamic_update_slice(keys, keys_mine, (0, core * half))
    keys = lax.dynamic_update_slice(keys, keys_other, (0, half - core * half))
    scaled = (back_mine + back_other) * gain_vec
    centre = jnp.mean(scaled * normed, axis=-1, keepdims=True)
    grads = (inverse * (scaled - normed * centre)).astype(jnp.bfloat16)
    return (keys[None], grads[None], new_params, new_momentum)


def solution(mesh):
    fine = Mesh(mesh.devices.reshape(tuple(SIZES.values())), tuple(SIZES))
    in_specs = (
        P(REPLICA, FSDP, None),
        P(REPLICA, None),
        P(REPLICA, FSDP, None),
        P(FSDP, None),
        P(REPLICA, FSDP, None),
        P(FSDP, None),
        P(),
    )
    out_specs = (
        P(REPLICA, FSDP, None),
        P(REPLICA, FSDP, None),
        P(FSDP, None),
        P(FSDP, None),
    )
    return jax.shard_map(body, mesh=fine, in_specs=in_specs, out_specs=out_specs, check_vma=False)
```

```python
import math

import jax
import jax.numpy as jnp
import numpy as np
from jax import lax
from jax.experimental import pallas as pl
from jax.experimental.pallas import tpu as pltpu
from jax.sharding import Mesh, PartitionSpec as P

HB = 128


NORM_EPS = 1e-06
OUTER_MU = 0.9
OUTER_LR = 0.7
CLIP_LEVEL = 2.0

REPLICA = ("yh", "core")
FSDP = ("y1", "y0", "zh", "z0", "x1", "x0")
SIZES = {"yh": 2, "core": 2, "y1": 2, "y0": 2, "zh": 8, "z0": 2, "x1": 2, "x0": 2}
AXES = tuple(SIZES)


def signs():
    common = lax.broadcasted_iota(jnp.int32, (HB, HB), 0) & lax.broadcasted_iota(jnp.int32, (HB, HB), 1)
    for shift in (4, 2, 1):
        common = common ^ (common >> shift)
    return (1 - 2 * (common & 1)).astype(jnp.float32).astype(jnp.bfloat16)


def rotate(values, matrix):
    total = None
    rest = values
    for _ in range(3):
        part = rest.astype(jnp.bfloat16)
        rest = rest - part.astype(jnp.float32)
        product = jnp.dot(part, matrix, preferred_element_type=jnp.float32)
        total = product if total is None else total + product
    return total * (1.0 / math.sqrt(HB))


def update_kernel(local_ref, global_ref, moment_ref, bits_ref, weight_ref, pseudo_ref):
    replicas, row_count, width = local_ref.shape
    count = width // HB
    matrix = signs()
    sign_vec = (2 * bits_ref[...] - 1).astype(jnp.float32)
    global_rows = global_ref[...]
    pieces = []
    for replica in range(replicas):
        drift = (global_rows - local_ref[replica].astype(jnp.float32)) * sign_vec
        pieces += [drift[:, at * HB : (at + 1) * HB] for at in range(count)]
    rotated = rotate(jnp.concatenate(pieces, axis=0), matrix)
    block_scale = jnp.mean(jnp.abs(rotated), axis=-1, keepdims=True) + NORM_EPS
    terms = jnp.clip(rotated / block_scale, -CLIP_LEVEL, CLIP_LEVEL) * block_scale
    terms = terms.astype(jnp.bfloat16).astype(jnp.float32)
    rows = count * row_count
    summed = terms[:rows]
    for replica in range(1, replicas):
        summed = summed + terms[replica * rows : (replica + 1) * rows]
    restored = rotate(summed / replicas, matrix)
    restored = jnp.concatenate([restored[at * row_count : (at + 1) * row_count] for at in range(count)], axis=1)
    pseudo = restored * sign_vec
    params, _ = step(global_rows, moment_ref[...], pseudo)
    pseudo_ref[...] = pseudo
    weight_ref[...] = params.astype(jnp.bfloat16)


def step(global_rows, moment_rows, pseudo):
    fresh_moment = OUTER_MU * moment_rows + pseudo
    fresh_params = global_rows - OUTER_LR * (pseudo + OUTER_MU * fresh_moment)
    return (fresh_params, fresh_moment)


def outer_update(all_local, global_params, momentum, sign_bits):
    row_count, width = global_params.shape
    return pl.pallas_call(
        update_kernel,
        out_shape=(
            jax.ShapeDtypeStruct((row_count, width), jnp.bfloat16),
            jax.ShapeDtypeStruct((row_count, width), jnp.float32),
        ),
        in_specs=[pl.BlockSpec(memory_space=pltpu.VMEM)] * 4,
        out_specs=[pl.BlockSpec(memory_space=pltpu.VMEM)] * 2,
        compiler_params=pltpu.CompilerParams(vmem_limit_bytes=4 * 1024 * 1024),
        cost_estimate=pl.CostEstimate(flops=20_000_000, bytes_accessed=250_000, transcendentals=0),
    )(all_local, global_params, momentum, sign_bits.reshape(1, width))


CHUNK = 512
PIECE_AXES = ("y0", "z0", "x0", "y1", "x1", "zh")


def pieces_of(chunk, row_count):
    order = ("y1", "y0", "zh", "z0", "x1", "x0")
    sizes = [SIZES[axis] for axis in order]
    count = CHUNK // row_count
    for piece in range(chunk * count, (chunk + 1) * count):
        at = dict(zip(order, np.unravel_index(piece, sizes)))
        yield tuple(int(at[axis]) for axis in PIECE_AXES)


def tail_kernel(core_ref, weight_ref, cot_ref, back_ref, hidden_ref, tokens_ref, inverse_ref, gain_ref, mine_ref, keys_out, grads_out, scaled_ref, keys_ref, grads_ref, sems):
    tokens, width = tokens_ref.shape
    row_count, half = weight_ref.shape[-2:]
    chunks = width // CHUNK
    cotangent = cot_ref[...]
    keys = jnp.zeros((tokens, half), jnp.float32)
    total = jnp.zeros((tokens, 1), jnp.float32)
    for chunk in range(chunks):
        columns = slice(chunk * CHUNK, (chunk + 1) * CHUNK)
        rows = jnp.concatenate([weight_ref[at] for at in pieces_of(chunk, row_count)], axis=0)
        back = back_ref[:, columns] + lax.dot_general(
            cotangent, rows, (((1,), (1,)), ((), ())), preferred_element_type=jnp.float32
        )
        keys = keys + jnp.dot(hidden_ref[:, columns], rows, preferred_element_type=jnp.float32)
        scaled = back * gain_ref[:, columns]
        scaled_ref[:, columns] = scaled
        total = total + jnp.sum(scaled * tokens_ref[:, columns].astype(jnp.float32), axis=1, keepdims=True)
    other = keys.astype(jnp.bfloat16).astype(jnp.float32)
    mine = mine_ref[...].astype(jnp.float32)
    first = core_ref[0] == 0
    keys_ref[:, :half] = jnp.where(first, mine, other).astype(jnp.bfloat16)
    keys_ref[:, half:] = jnp.where(first, other, mine).astype(jnp.bfloat16)
    copies = [pltpu.make_async_copy(keys_ref, keys_out, sems.at[chunks])]
    copies[0].start()
    inverse = inverse_ref[...]
    centre = inverse * total / width
    factor = inverse * inverse * centre
    for chunk in range(chunks):
        columns = slice(chunk * CHUNK, (chunk + 1) * CHUNK)
        grads = inverse * scaled_ref[:, columns] - factor * tokens_ref[:, columns].astype(jnp.float32)
        grads_ref[:, columns] = grads.astype(jnp.bfloat16)
        copy = pltpu.make_async_copy(grads_ref.at[:, columns], grads_out.at[:, columns], sems.at[chunk])
        copy.start()
        copies.append(copy)
    for copy in copies:
        copy.wait()


def tail(core, weight, cotangent, back, hidden, tokens, inverse, gain, keys_mine):
    count, width = tokens.shape
    half = keys_mine.shape[1]
    vmem = pl.BlockSpec(memory_space=pltpu.VMEM)
    return pl.pallas_call(
        tail_kernel,
        out_shape=(
            jax.ShapeDtypeStruct((count, 2 * half), jnp.bfloat16),
            jax.ShapeDtypeStruct((count, width), jnp.bfloat16),
        ),
        in_specs=[pl.BlockSpec(memory_space=pltpu.SMEM)] + [vmem] * 8,
        out_specs=[pl.BlockSpec(memory_space=pltpu.HBM)] * 2,
        scratch_shapes=[
            pltpu.VMEM((count, width), jnp.float32),
            pltpu.VMEM((count, 2 * half), jnp.bfloat16),
            pltpu.VMEM((count, width), jnp.bfloat16),
            pltpu.SemaphoreType.DMA((width // CHUNK + 1,)),
        ],
        compiler_params=pltpu.CompilerParams(vmem_limit_bytes=20 * 1024 * 1024),
        cost_estimate=pl.CostEstimate(flops=900_000_000, bytes_accessed=12_000_000, transcendentals=0),
    )(core.reshape(1), weight, cotangent, back, hidden, tokens, inverse, gain, keys_mine)


def cubes():
    groups = []
    for core in range(2):
        for y in range(0, 8, 2):
            for z in range(0, 16, 2):
                for x in range(0, 4, 2):
                    group = []
                    for odd in np.ndindex(2, 2, 2):
                        step = [bit * (1 - 2 * core) for bit in odd]
                        y_at, z_at, x_at = (y + step[0]) % 8, (z + step[1]) % 16, (x + step[2]) % 4
                        group.append((((y_at // 4 * 2 + core) * 4 + y_at % 4) * 16 + z_at) * 4 + x_at)
                    groups.append(group)
    return groups


def gather(block, axes, count, groups=None):
    copies = jnp.broadcast_to(block[None], (count,) + block.shape)
    return lax.all_to_all(copies, axes, 0, 0, axis_index_groups=groups, tiled=True)


def body(tokens, gain, key_cotangent, global_params, local_params, momentum, sign_bits):
    all_local = gather(local_params[0], REPLICA, 4)
    weight_part, pseudo = outer_update(all_local, global_params, momentum, sign_bits)
    row_count, width = global_params.shape

    half = width // 2
    core = lax.axis_index("core")
    mine = jnp.where(core == 0, weight_part[:, :half], weight_part[:, half:])
    got = gather(mine, ("zh",), 8)
    got = gather(got, ("y1", "x1"), 4)
    got = gather(got, AXES, 8, cubes())
    got = got.reshape(tuple(SIZES[axis] for axis in PIECE_AXES) + (row_count, half))
    other = lax.ppermute(got, "core", [(0, 1), (1, 0)])
    weight = got.transpose(3, 0, 5, 1, 4, 2, 6, 7).reshape(-1, half)

    pseudo, outer, moment, _ = lax.optimization_barrier((pseudo, global_params, momentum, got))
    new_params, new_momentum = step(outer, moment, pseudo)
    tok_float = tokens[0].astype(jnp.float32)
    inverse = lax.rsqrt(jnp.mean(tok_float * tok_float, axis=-1, keepdims=True) + NORM_EPS)
    hidden = (tok_float * inverse * gain[0]).astype(jnp.bfloat16)
    hidden = lax.optimization_barrier(hidden)
    low, high = key_cotangent[0][:, :half], key_cotangent[0][:, half:]
    cot_mine = jnp.where(core == 0, low, high)
    cot_other = jnp.where(core == 0, high, low)
    keys_mine = jnp.dot(hidden, weight, preferred_element_type=jnp.float32).astype(jnp.bfloat16)
    back = lax.dot_general(cot_mine, weight, (((1,), (1,)), ((), ())), preferred_element_type=jnp.float32)
    keys, grads = tail(core, other, cot_other, back, hidden, tokens[0], inverse, gain, keys_mine)
    return (keys[None], grads[None], new_params, new_momentum)


def solution(mesh):
    fine = Mesh(mesh.devices.reshape(tuple(SIZES.values())), tuple(SIZES))
    in_specs = (
        P(REPLICA, FSDP, None),
        P(REPLICA, None),
        P(REPLICA, FSDP, None),
        P(FSDP, None),
        P(REPLICA, FSDP, None),
        P(FSDP, None),
        P(),
    )
    out_specs = (
        P(REPLICA, FSDP, None),
        P(REPLICA, FSDP, None),
        P(FSDP, None),
        P(FSDP, None),
    )
    return jax.shard_map(body, mesh=fine, in_specs=in_specs, out_specs=out_specs, check_vma=False)
```

```python
import math

import jax
import jax.numpy as jnp
import numpy as np
from jax import lax
from jax.experimental import pallas as pl
from jax.experimental.pallas import tpu as pltpu
from jax.sharding import Mesh, PartitionSpec as P

HB = 128


NORM_EPS = 1e-06
OUTER_MU = 0.9
OUTER_LR = 0.7
CLIP_LEVEL = 2.0

REPLICA = ("yh", "core")
FSDP = ("y1", "y0", "zh", "z0", "x1", "x0")
SIZES = {"yh": 2, "core": 2, "y1": 2, "y0": 2, "zh": 8, "z0": 2, "x1": 2, "x0": 2}
AXES = tuple(SIZES)


def signs():
    common = lax.broadcasted_iota(jnp.int32, (HB, HB), 0) & lax.broadcasted_iota(jnp.int32, (HB, HB), 1)
    for shift in (4, 2, 1):
        common = common ^ (common >> shift)
    return (1 - 2 * (common & 1)).astype(jnp.float32).astype(jnp.bfloat16)


def rotate(values, matrix):
    total = None
    rest = values
    for _ in range(3):
        part = rest.astype(jnp.bfloat16)
        rest = rest - part.astype(jnp.float32)
        product = jnp.dot(part, matrix, preferred_element_type=jnp.float32)
        total = product if total is None else total + product
    return total * (1.0 / math.sqrt(HB))


def update_kernel(local_ref, held_ref, weight_ref, pseudo_ref):
    replicas, row_count, width = local_ref.shape
    count = width // HB
    matrix = signs()
    sign_vec = held_ref[2]
    global_rows = held_ref[0]
    pieces = []
    for replica in range(replicas):
        drift = (global_rows - local_ref[replica].astype(jnp.float32)) * sign_vec
        pieces += [drift[:, at * HB : (at + 1) * HB] for at in range(count)]
    rotated = rotate(jnp.concatenate(pieces, axis=0), matrix)
    block_scale = jnp.mean(jnp.abs(rotated), axis=-1, keepdims=True) + NORM_EPS
    terms = jnp.clip(rotated / block_scale, -CLIP_LEVEL, CLIP_LEVEL) * block_scale
    terms = terms.astype(jnp.bfloat16).astype(jnp.float32)
    rows = count * row_count
    summed = terms[:rows]
    for replica in range(1, replicas):
        summed = summed + terms[replica * rows : (replica + 1) * rows]
    restored = rotate(summed / replicas, matrix)
    restored = jnp.concatenate([restored[at * row_count : (at + 1) * row_count] for at in range(count)], axis=1)
    pseudo = restored * sign_vec
    params, _ = step(global_rows, held_ref[1], pseudo)
    pseudo_ref[...] = pseudo
    weight_ref[...] = params.astype(jnp.bfloat16)


def step(global_rows, moment_rows, pseudo):
    fresh_moment = OUTER_MU * moment_rows + pseudo
    fresh_params = global_rows - OUTER_LR * (pseudo + OUTER_MU * fresh_moment)
    return (fresh_params, fresh_moment)


def outer_update(all_local, held):
    row_count, width = held.shape[1:]
    return pl.pallas_call(
        update_kernel,
        out_shape=(
            jax.ShapeDtypeStruct((row_count, width), jnp.bfloat16),
            jax.ShapeDtypeStruct((row_count, width), jnp.float32),
        ),
        in_specs=[pl.BlockSpec(memory_space=pltpu.VMEM)] * 2,
        out_specs=[pl.BlockSpec(memory_space=pltpu.VMEM)] * 2,
        compiler_params=pltpu.CompilerParams(vmem_limit_bytes=4 * 1024 * 1024),
        cost_estimate=pl.CostEstimate(flops=20_000_000, bytes_accessed=250_000, transcendentals=0),
    )(all_local, held)


CHUNK = 512
PIECE_AXES = ("y0", "z0", "x0", "y1", "x1", "zh")


def pieces_of(chunk, row_count):
    order = ("y1", "y0", "zh", "z0", "x1", "x0")
    sizes = [SIZES[axis] for axis in order]
    count = CHUNK // row_count
    for piece in range(chunk * count, (chunk + 1) * count):
        at = dict(zip(order, np.unravel_index(piece, sizes)))
        yield tuple(int(at[axis]) for axis in PIECE_AXES)


def columns_of(core, half):
    return pl.ds(pl.multiple_of(core * half, half), half)


def own_kernel(core_ref, weight_ref, cot_ref, tokens_ref, gain_ref, held_ref, pseudo_ref, back_ref, hidden_ref, inverse_ref, keys_ref, params_ref, fresh_ref):
    tokens, width = tokens_ref.shape
    row_count, half = weight_ref.shape[-2:]
    parts = [slice(at, at + CHUNK) for at in range(0, width, CHUNK)]
    total = jnp.zeros((tokens, 1), jnp.float32)
    for columns in parts:
        values = tokens_ref[:, columns].astype(jnp.float32)
        total = total + jnp.sum(values * values, axis=1, keepdims=True)
    inverse = lax.rsqrt(total / width + NORM_EPS)
    inverse_ref[...] = inverse
    cotangent = cot_ref[:, columns_of(core_ref[0], half)]
    keys = jnp.zeros((tokens, half), jnp.float32)
    for chunk, columns in enumerate(parts):
        rows = jnp.concatenate([weight_ref[at] for at in pieces_of(chunk, row_count)], axis=0)
        back_ref[:, columns] = lax.dot_general(
            cotangent, rows, (((1,), (1,)), ((), ())), preferred_element_type=jnp.float32
        )
        hidden = (tokens_ref[:, columns].astype(jnp.float32) * inverse * gain_ref[:, columns]).astype(jnp.bfloat16)
        hidden_ref[:, columns] = hidden
        keys = keys + jnp.dot(hidden, rows, preferred_element_type=jnp.float32)
    keys_ref[...] = keys.astype(jnp.bfloat16)
    params, fresh = step(held_ref[0], held_ref[1], pseudo_ref[...])
    params_ref[...] = params
    fresh_ref[...] = fresh


def own_half(core, weight, cotangent, tokens, gain, held, pseudo):
    count, width = tokens.shape
    half = weight.shape[-1]
    vmem = pl.BlockSpec(memory_space=pltpu.VMEM)
    return pl.pallas_call(
        own_kernel,
        out_shape=(
            jax.ShapeDtypeStruct((count, width), jnp.float32),
            jax.ShapeDtypeStruct((count, width), jnp.bfloat16),
            jax.ShapeDtypeStruct((count, 1), jnp.float32),
            jax.ShapeDtypeStruct((count, half), jnp.bfloat16),
            jax.ShapeDtypeStruct(pseudo.shape, jnp.float32),
            jax.ShapeDtypeStruct(pseudo.shape, jnp.float32),
        ),
        in_specs=[pl.BlockSpec(memory_space=pltpu.SMEM)] + [vmem] * 6,
        out_specs=[vmem] * 6,
        compiler_params=pltpu.CompilerParams(vmem_limit_bytes=24 * 1024 * 1024),
        cost_estimate=pl.CostEstimate(flops=900_000_000, bytes_accessed=12_000_000, transcendentals=0),
    )(core.reshape(1), weight, cotangent, tokens, gain, held, pseudo)


def tail_kernel(core_ref, weight_ref, cot_ref, back_ref, hidden_ref, tokens_ref, inverse_ref, gain_ref, mine_ref, keys_out, grads_out, scaled_ref, keys_ref, grads_ref, sems):
    tokens, width = tokens_ref.shape
    row_count, half = weight_ref.shape[-2:]
    parts = [slice(at, at + CHUNK) for at in range(0, width, CHUNK)]
    core = core_ref[0]
    cotangent = cot_ref[:, columns_of(1 - core, half)]
    keys = jnp.zeros((tokens, half), jnp.float32)
    total = jnp.zeros((tokens, 1), jnp.float32)
    for chunk, columns in enumerate(parts):
        rows = jnp.concatenate([weight_ref[at] for at in pieces_of(chunk, row_count)], axis=0)
        back = back_ref[:, columns] + lax.dot_general(
            cotangent, rows, (((1,), (1,)), ((), ())), preferred_element_type=jnp.float32
        )
        keys = keys + jnp.dot(hidden_ref[:, columns], rows, preferred_element_type=jnp.float32)
        scaled = back * gain_ref[:, columns]
        scaled_ref[:, columns] = scaled
        total = total + jnp.sum(scaled * tokens_ref[:, columns].astype(jnp.float32), axis=1, keepdims=True)
    keys_ref[:, columns_of(core, half)] = mine_ref[...]
    keys_ref[:, columns_of(1 - core, half)] = keys.astype(jnp.bfloat16)
    copies = [pltpu.make_async_copy(keys_ref, keys_out, sems.at[len(parts)])]
    copies[0].start()
    inverse = inverse_ref[...]
    centre = inverse * total / width
    factor = inverse * inverse * centre
    for chunk, columns in enumerate(parts):
        grads = inverse * scaled_ref[:, columns] - factor * tokens_ref[:, columns].astype(jnp.float32)
        grads_ref[:, columns] = grads.astype(jnp.bfloat16)
        copy = pltpu.make_async_copy(grads_ref.at[:, columns], grads_out.at[:, columns], sems.at[chunk])
        copy.start()
        copies.append(copy)
    for copy in copies:
        copy.wait()


def tail(core, weight, cotangent, back, hidden, tokens, inverse, gain, keys_mine):
    count, width = tokens.shape
    half = keys_mine.shape[1]
    vmem = pl.BlockSpec(memory_space=pltpu.VMEM)
    return pl.pallas_call(
        tail_kernel,
        out_shape=(
            jax.ShapeDtypeStruct((count, 2 * half), jnp.bfloat16),
            jax.ShapeDtypeStruct((count, width), jnp.bfloat16),
        ),
        in_specs=[pl.BlockSpec(memory_space=pltpu.SMEM)] + [vmem] * 8,
        out_specs=[pl.BlockSpec(memory_space=pltpu.HBM)] * 2,
        scratch_shapes=[
            pltpu.VMEM((count, width), jnp.float32),
            pltpu.VMEM((count, 2 * half), jnp.bfloat16),
            pltpu.VMEM((count, width), jnp.bfloat16),
            pltpu.SemaphoreType.DMA((width // CHUNK + 1,)),
        ],
        compiler_params=pltpu.CompilerParams(vmem_limit_bytes=20 * 1024 * 1024),
        cost_estimate=pl.CostEstimate(flops=900_000_000, bytes_accessed=12_000_000, transcendentals=0),
    )(core.reshape(1), weight, cotangent, back, hidden, tokens, inverse, gain, keys_mine)


def cubes():
    groups = []
    for core in range(2):
        for y in range(0, 8, 2):
            for z in range(0, 16, 2):
                for x in range(0, 4, 2):
                    group = []
                    for odd in np.ndindex(2, 2, 2):
                        step = [bit * (1 - 2 * core) for bit in odd]
                        y_at, z_at, x_at = (y + step[0]) % 8, (z + step[1]) % 16, (x + step[2]) % 4
                        group.append((((y_at // 4 * 2 + core) * 4 + y_at % 4) * 16 + z_at) * 4 + x_at)
                    groups.append(group)
    return groups


def gather(block, axes, count, groups=None):
    copies = jnp.broadcast_to(block[None], (count,) + block.shape)
    return lax.all_to_all(copies, axes, 0, 0, axis_index_groups=groups, tiled=True)


def body(tokens, gain, key_cotangent, global_params, local_params, momentum, sign_bits):
    all_local = gather(local_params[0], REPLICA, 4)
    row_count, width = global_params.shape
    sign_vec = jnp.broadcast_to((2 * sign_bits - 1).astype(jnp.float32), (row_count, width))
    held = lax.optimization_barrier(jnp.stack([global_params, momentum, sign_vec]))
    weight_part, pseudo = outer_update(all_local, held)

    half = width // 2
    core = lax.axis_index("core")
    mine = jnp.where(core == 0, weight_part[:, :half], weight_part[:, half:])
    got = gather(mine, ("zh",), 8)
    got = gather(got, ("y1", "x1"), 4)
    got = gather(got, AXES, 8, cubes())
    got = got.reshape(tuple(SIZES[axis] for axis in PIECE_AXES) + (row_count, half))
    other = lax.ppermute(got, "core", [(0, 1), (1, 0)])

    rows, cotangent = tokens[0], key_cotangent[0]
    own = own_half(core, got, cotangent, rows, gain, held, pseudo)
    back, hidden, inverse, keys_mine, new_params, new_momentum = own
    keys, grads = tail(core, other, cotangent, back, hidden, rows, inverse, gain, keys_mine)
    return (keys[None], grads[None], new_params, new_momentum)


def solution(mesh):
    fine = Mesh(mesh.devices.reshape(tuple(SIZES.values())), tuple(SIZES))
    in_specs = (
        P(REPLICA, FSDP, None),
        P(REPLICA, None),
        P(REPLICA, FSDP, None),
        P(FSDP, None),
        P(REPLICA, FSDP, None),
        P(FSDP, None),
        P(),
    )
    out_specs = (
        P(REPLICA, FSDP, None),
        P(REPLICA, FSDP, None),
        P(FSDP, None),
        P(FSDP, None),
    )
    return jax.shard_map(body, mesh=fine, in_specs=in_specs, out_specs=out_specs, check_vma=False)
```

```python
import math

import jax
import jax.numpy as jnp
import numpy as np
from jax import lax
from jax.experimental import pallas as pl
from jax.experimental.pallas import tpu as pltpu
from jax.sharding import Mesh, PartitionSpec as P

HB = 128


NORM_EPS = 1e-06
OUTER_MU = 0.9
OUTER_LR = 0.7
CLIP_LEVEL = 2.0

REPLICA = ("yh", "core")
FSDP = ("y1", "y0", "zh", "z0", "x1", "x0")
SIZES = {"yh": 2, "core": 2, "y1": 2, "y0": 2, "zh": 8, "z0": 2, "x1": 2, "x0": 2}
AXES = tuple(SIZES)


def signs():
    common = lax.broadcasted_iota(jnp.int32, (HB, HB), 0) & lax.broadcasted_iota(jnp.int32, (HB, HB), 1)
    for shift in (4, 2, 1):
        common = common ^ (common >> shift)
    return (1 - 2 * (common & 1)).astype(jnp.float32).astype(jnp.bfloat16)


def rotate(values, matrix):
    total = None
    rest = values
    for _ in range(3):
        part = rest.astype(jnp.bfloat16)
        rest = rest - part.astype(jnp.float32)
        product = jnp.dot(part, matrix, preferred_element_type=jnp.float32)
        total = product if total is None else total + product
    return total * (1.0 / math.sqrt(HB))


def update_kernel(local_ref, held_ref, weight_ref, pseudo_ref):
    replicas, row_count, width = local_ref.shape
    count = width // HB
    matrix = signs()
    sign_vec = held_ref[2]
    global_rows = held_ref[0]
    pieces = []
    for replica in range(replicas):
        drift = (global_rows - local_ref[replica].astype(jnp.float32)) * sign_vec
        pieces += [drift[:, at * HB : (at + 1) * HB] for at in range(count)]
    rotated = rotate(jnp.concatenate(pieces, axis=0), matrix)
    block_scale = jnp.mean(jnp.abs(rotated), axis=-1, keepdims=True) + NORM_EPS
    terms = jnp.clip(rotated / block_scale, -CLIP_LEVEL, CLIP_LEVEL) * block_scale
    terms = terms.astype(jnp.bfloat16).astype(jnp.float32)
    rows = count * row_count
    summed = terms[:rows]
    for replica in range(1, replicas):
        summed = summed + terms[replica * rows : (replica + 1) * rows]
    restored = rotate(summed / replicas, matrix)
    restored = jnp.concatenate([restored[at * row_count : (at + 1) * row_count] for at in range(count)], axis=1)
    pseudo = restored * sign_vec
    params, _ = step(global_rows, held_ref[1], pseudo)
    pseudo_ref[...] = pseudo
    weight_ref[...] = params.astype(jnp.bfloat16)


def step(global_rows, moment_rows, pseudo):
    fresh_moment = OUTER_MU * moment_rows + pseudo
    fresh_params = global_rows - OUTER_LR * (pseudo + OUTER_MU * fresh_moment)
    return (fresh_params, fresh_moment)


def outer_update(all_local, held):
    row_count, width = held.shape[1:]
    return pl.pallas_call(
        update_kernel,
        out_shape=(
            jax.ShapeDtypeStruct((row_count, width), jnp.bfloat16),
            jax.ShapeDtypeStruct((row_count, width), jnp.float32),
        ),
        in_specs=[pl.BlockSpec(memory_space=pltpu.VMEM)] * 2,
        out_specs=[pl.BlockSpec(memory_space=pltpu.VMEM)] * 2,
        compiler_params=pltpu.CompilerParams(vmem_limit_bytes=4 * 1024 * 1024),
        cost_estimate=pl.CostEstimate(flops=20_000_000, bytes_accessed=250_000, transcendentals=0),
    )(all_local, held)


CHUNK = 512
PIECE_AXES = ("y0", "z0", "x0", "y1", "x1", "zh")


def pieces_of(chunk, row_count):
    order = ("y1", "y0", "zh", "z0", "x1", "x0")
    sizes = [SIZES[axis] for axis in order]
    count = CHUNK // row_count
    for piece in range(chunk * count, (chunk + 1) * count):
        at = dict(zip(order, np.unravel_index(piece, sizes)))
        yield tuple(int(at[axis]) for axis in PIECE_AXES)


def columns_of(core, half):
    return pl.ds(pl.multiple_of(core * half, half), half)


def own_kernel(core_ref, weight_ref, cot_ref, tokens_ref, gain_ref, held_ref, pseudo_ref, back_ref, hidden_ref, inverse_ref, keys_ref, params_ref, fresh_ref):
    tokens, width = tokens_ref.shape
    row_count, half = weight_ref.shape[-2:]
    parts = [slice(at, at + CHUNK) for at in range(0, width, CHUNK)]
    total = jnp.zeros((tokens, 1), jnp.float32)
    for columns in parts:
        values = tokens_ref[:, columns].astype(jnp.float32)
        total = total + jnp.sum(values * values, axis=1, keepdims=True)
    inverse = lax.rsqrt(total / width + NORM_EPS)
    inverse_ref[...] = inverse
    cotangent = cot_ref[:, columns_of(core_ref[0], half)]
    keys = jnp.zeros((tokens, half), jnp.float32)
    for chunk, columns in enumerate(parts):
        rows = jnp.concatenate([weight_ref[at] for at in pieces_of(chunk, row_count)], axis=0)
        back_ref[:, columns] = lax.dot_general(
            cotangent, rows, (((1,), (1,)), ((), ())), preferred_element_type=jnp.float32
        )
        hidden = (tokens_ref[:, columns].astype(jnp.float32) * inverse * gain_ref[:, columns]).astype(jnp.bfloat16)
        hidden_ref[:, columns] = hidden
        keys = keys + jnp.dot(hidden, rows, preferred_element_type=jnp.float32)
    keys_ref[...] = keys.astype(jnp.bfloat16)
    params, fresh = step(held_ref[0], held_ref[1], pseudo_ref[...])
    params_ref[...] = params
    fresh_ref[...] = fresh


def own_half(core, weight, cotangent, tokens, gain, held, pseudo):
    count, width = tokens.shape
    half = weight.shape[-1]
    vmem = pl.BlockSpec(memory_space=pltpu.VMEM)
    return pl.pallas_call(
        own_kernel,
        out_shape=(
            jax.ShapeDtypeStruct((count, width), jnp.float32),
            jax.ShapeDtypeStruct((count, width), jnp.bfloat16),
            jax.ShapeDtypeStruct((count, 1), jnp.float32),
            jax.ShapeDtypeStruct((count, half), jnp.bfloat16),
            jax.ShapeDtypeStruct(pseudo.shape, jnp.float32),
            jax.ShapeDtypeStruct(pseudo.shape, jnp.float32),
        ),
        in_specs=[pl.BlockSpec(memory_space=pltpu.SMEM)] + [vmem] * 6,
        out_specs=[vmem] * 6,
        compiler_params=pltpu.CompilerParams(vmem_limit_bytes=24 * 1024 * 1024),
        cost_estimate=pl.CostEstimate(flops=900_000_000, bytes_accessed=12_000_000, transcendentals=0),
    )(core.reshape(1), weight, cotangent, tokens, gain, held, pseudo)


def tail_kernel(core_ref, weight_ref, cot_ref, back_ref, hidden_ref, tokens_ref, inverse_ref, gain_ref, mine_ref, keys_out, grads_out, scaled_ref, keys_ref, grads_ref, sems):
    tokens, width = tokens_ref.shape
    row_count, half = weight_ref.shape[-2:]
    parts = [slice(at, at + CHUNK) for at in range(0, width, CHUNK)]
    core = core_ref[0]
    cotangent = cot_ref[:, columns_of(1 - core, half)]
    keys = jnp.zeros((tokens, half), jnp.float32)
    total = jnp.zeros((tokens, HB), jnp.float32)
    for chunk, columns in enumerate(parts):
        rows = jnp.concatenate([weight_ref[at] for at in pieces_of(chunk, row_count)], axis=0)
        back = back_ref[:, columns] + lax.dot_general(
            cotangent, rows, (((1,), (1,)), ((), ())), preferred_element_type=jnp.float32
        )
        keys = keys + jnp.dot(hidden_ref[:, columns], rows, preferred_element_type=jnp.float32)
        scaled = back * gain_ref[:, columns]
        scaled_ref[:, columns] = scaled
        product = scaled * tokens_ref[:, columns].astype(jnp.float32)
        for at in range(0, CHUNK, HB):
            total = total + product[:, at : at + HB]
    keys_ref[:, columns_of(core, half)] = mine_ref[...]
    keys_ref[:, columns_of(1 - core, half)] = keys.astype(jnp.bfloat16)
    copies = [pltpu.make_async_copy(keys_ref, keys_out, sems.at[len(parts)])]
    copies[0].start()
    inverse = inverse_ref[...]
    centre = inverse * jnp.sum(total, axis=1, keepdims=True) / width
    factor = inverse * inverse * centre
    for chunk, columns in enumerate(parts):
        grads = inverse * scaled_ref[:, columns] - factor * tokens_ref[:, columns].astype(jnp.float32)
        grads_ref[:, columns] = grads.astype(jnp.bfloat16)
        copy = pltpu.make_async_copy(grads_ref.at[:, columns], grads_out.at[:, columns], sems.at[chunk])
        copy.start()
        copies.append(copy)
    for copy in copies:
        copy.wait()


def tail(core, weight, cotangent, back, hidden, tokens, inverse, gain, keys_mine):
    count, width = tokens.shape
    half = keys_mine.shape[1]
    vmem = pl.BlockSpec(memory_space=pltpu.VMEM)
    return pl.pallas_call(
        tail_kernel,
        out_shape=(
            jax.ShapeDtypeStruct((count, 2 * half), jnp.bfloat16),
            jax.ShapeDtypeStruct((count, width), jnp.bfloat16),
        ),
        in_specs=[pl.BlockSpec(memory_space=pltpu.SMEM)] + [vmem] * 8,
        out_specs=[pl.BlockSpec(memory_space=pltpu.HBM)] * 2,
        scratch_shapes=[
            pltpu.VMEM((count, width), jnp.float32),
            pltpu.VMEM((count, 2 * half), jnp.bfloat16),
            pltpu.VMEM((count, width), jnp.bfloat16),
            pltpu.SemaphoreType.DMA((width // CHUNK + 1,)),
        ],
        compiler_params=pltpu.CompilerParams(vmem_limit_bytes=20 * 1024 * 1024),
        cost_estimate=pl.CostEstimate(flops=900_000_000, bytes_accessed=12_000_000, transcendentals=0),
    )(core.reshape(1), weight, cotangent, back, hidden, tokens, inverse, gain, keys_mine)


def place(core, y, z, x):
    return (((y // 4 * 2 + core) * 4 + y % 4) * 16 + z) * 4 + x


def squares():
    groups = []
    for core in range(2):
        for y in (0, 1, 4, 5):
            pair = (y, (y + 2 - 4 * core) % 8)
            for z in range(16):
                for x in range(2):
                    groups.append([place(core, y_at, z, x_at) for y_at in pair for x_at in (x, x + 2)])
    return groups


def cubes():
    groups = []
    for core in range(2):
        for y in range(0, 8, 2):
            for z in range(0, 16, 2):
                for x in range(0, 4, 2):
                    group = []
                    for odd in np.ndindex(2, 2, 2):
                        step = [bit * (1 - 2 * core) for bit in odd]
                        group.append(place(core, (y + step[0]) % 8, (z + step[1]) % 16, (x + step[2]) % 4))
                    groups.append(group)
    return groups


def gather(block, axes, count, groups=None):
    copies = jnp.broadcast_to(block[None], (count,) + block.shape)
    return lax.all_to_all(copies, axes, 0, 0, axis_index_groups=groups, tiled=True)


def body(tokens, gain, key_cotangent, global_params, local_params, momentum, sign_bits):
    all_local = gather(local_params[0], REPLICA, 4)
    row_count, width = global_params.shape
    sign_vec = jnp.broadcast_to((2 * sign_bits - 1).astype(jnp.float32), (row_count, width))
    held = lax.optimization_barrier(jnp.stack([global_params, momentum, sign_vec]))
    weight_part, pseudo = outer_update(all_local, held)

    half = width // 2
    core = lax.axis_index("core")
    mine = jnp.where(core == 0, weight_part[:, :half], weight_part[:, half:])
    got = gather(mine, ("zh",), 8)
    got = gather(got, AXES, 4, squares())
    got = gather(got, AXES, 8, cubes())
    got = got.reshape(tuple(SIZES[axis] for axis in PIECE_AXES) + (row_count, half))
    other = lax.ppermute(got, "core", [(0, 1), (1, 0)])

    rows, cotangent = tokens[0], key_cotangent[0]
    own = own_half(core, got, cotangent, rows, gain, held, pseudo)
    back, hidden, inverse, keys_mine, new_params, new_momentum = own
    keys, grads = tail(core, other, cotangent, back, hidden, rows, inverse, gain, keys_mine)
    return (keys[None], grads[None], new_params, new_momentum)


def solution(mesh):
    fine = Mesh(mesh.devices.reshape(tuple(SIZES.values())), tuple(SIZES))
    in_specs = (
        P(REPLICA, FSDP, None),
        P(REPLICA, None),
        P(REPLICA, FSDP, None),
        P(FSDP, None),
        P(REPLICA, FSDP, None),
        P(FSDP, None),
        P(),
    )
    out_specs = (
        P(REPLICA, FSDP, None),
        P(REPLICA, FSDP, None),
        P(FSDP, None),
        P(FSDP, None),
    )
    return jax.shard_map(body, mesh=fine, in_specs=in_specs, out_specs=out_specs, check_vma=False)
```

```python
import math

import jax
import jax.numpy as jnp
import numpy as np
from jax import lax
from jax.experimental import pallas as pl
from jax.experimental.pallas import tpu as pltpu
from jax.sharding import Mesh, PartitionSpec as P

HB = 128


NORM_EPS = 1e-06
OUTER_MU = 0.9
OUTER_LR = 0.7
CLIP_LEVEL = 2.0

REPLICA = ("yh", "core")
FSDP = ("y1", "y0", "zh", "z0", "x1", "x0")
SIZES = {"yh": 2, "core": 2, "y1": 2, "y0": 2, "zh": 8, "z0": 2, "x1": 2, "x0": 2}
AXES = tuple(SIZES)


def signs():
    common = lax.broadcasted_iota(jnp.int32, (HB, HB), 0) & lax.broadcasted_iota(jnp.int32, (HB, HB), 1)
    for shift in (4, 2, 1):
        common = common ^ (common >> shift)
    return (1 - 2 * (common & 1)).astype(jnp.float32).astype(jnp.bfloat16)


def rotate(values, matrix):
    total = None
    rest = values
    for _ in range(3):
        part = rest.astype(jnp.bfloat16)
        rest = rest - part.astype(jnp.float32)
        product = jnp.dot(part, matrix, preferred_element_type=jnp.float32)
        total = product if total is None else total + product
    return total * (1.0 / math.sqrt(HB))


def update_kernel(local_ref, held_ref, weight_ref, pseudo_ref):
    replicas, row_count, width = local_ref.shape
    count = width // HB
    matrix = signs()
    sign_vec = held_ref[2]
    global_rows = held_ref[0]
    pieces = []
    for replica in range(replicas):
        drift = (global_rows - local_ref[replica].astype(jnp.float32)) * sign_vec
        pieces += [drift[:, at * HB : (at + 1) * HB] for at in range(count)]
    rotated = rotate(jnp.concatenate(pieces, axis=0), matrix)
    block_scale = jnp.mean(jnp.abs(rotated), axis=-1, keepdims=True) + NORM_EPS
    terms = jnp.clip(rotated / block_scale, -CLIP_LEVEL, CLIP_LEVEL) * block_scale
    terms = terms.astype(jnp.bfloat16).astype(jnp.float32)
    rows = count * row_count
    summed = terms[:rows]
    for replica in range(1, replicas):
        summed = summed + terms[replica * rows : (replica + 1) * rows]
    restored = rotate(summed / replicas, matrix)
    restored = jnp.concatenate([restored[at * row_count : (at + 1) * row_count] for at in range(count)], axis=1)
    pseudo = restored * sign_vec
    params, _ = step(global_rows, held_ref[1], pseudo)
    pseudo_ref[...] = pseudo
    weight_ref[...] = params.astype(jnp.bfloat16)


def step(global_rows, moment_rows, pseudo):
    fresh_moment = OUTER_MU * moment_rows + pseudo
    fresh_params = global_rows - OUTER_LR * (pseudo + OUTER_MU * fresh_moment)
    return (fresh_params, fresh_moment)


def outer_update(all_local, held):
    row_count, width = held.shape[1:]
    return pl.pallas_call(
        update_kernel,
        out_shape=(
            jax.ShapeDtypeStruct((row_count, width), jnp.bfloat16),
            jax.ShapeDtypeStruct((row_count, width), jnp.float32),
        ),
        in_specs=[pl.BlockSpec(memory_space=pltpu.VMEM)] * 2,
        out_specs=[pl.BlockSpec(memory_space=pltpu.VMEM)] * 2,
        compiler_params=pltpu.CompilerParams(vmem_limit_bytes=4 * 1024 * 1024),
        cost_estimate=pl.CostEstimate(flops=20_000_000, bytes_accessed=250_000, transcendentals=0),
    )(all_local, held)


CHUNK = 512
PIECE_AXES = ("y0", "z0", "x0", "y1", "zh", "x1")


def pieces_of(chunk, row_count):
    order = ("y1", "y0", "zh", "z0", "x1", "x0")
    sizes = [SIZES[axis] for axis in order]
    count = CHUNK // row_count
    for piece in range(chunk * count, (chunk + 1) * count):
        at = dict(zip(order, np.unravel_index(piece, sizes)))
        yield tuple(int(at[axis]) for axis in PIECE_AXES)


def columns_of(core, half):
    return pl.ds(pl.multiple_of(core * half, half), half)


def own_kernel(core_ref, weight_ref, cot_ref, tokens_ref, gain_ref, held_ref, pseudo_ref, back_ref, hidden_ref, inverse_ref, keys_ref, params_ref, fresh_ref):
    tokens, width = tokens_ref.shape
    row_count, half = weight_ref.shape[-2:]
    parts = [slice(at, at + CHUNK) for at in range(0, width, CHUNK)]
    total = jnp.zeros((tokens, 1), jnp.float32)
    for columns in parts:
        values = tokens_ref[:, columns].astype(jnp.float32)
        total = total + jnp.sum(values * values, axis=1, keepdims=True)
    inverse = lax.rsqrt(total / width + NORM_EPS)
    inverse_ref[...] = inverse
    cotangent = cot_ref[:, columns_of(core_ref[0], half)]
    keys = jnp.zeros((tokens, half), jnp.float32)
    for chunk, columns in enumerate(parts):
        rows = jnp.concatenate([weight_ref[at] for at in pieces_of(chunk, row_count)], axis=0)
        back_ref[:, columns] = lax.dot_general(
            cotangent, rows, (((1,), (1,)), ((), ())), preferred_element_type=jnp.float32
        )
        hidden = (tokens_ref[:, columns].astype(jnp.float32) * inverse * gain_ref[:, columns]).astype(jnp.bfloat16)
        hidden_ref[:, columns] = hidden
        keys = keys + jnp.dot(hidden, rows, preferred_element_type=jnp.float32)
    keys_ref[...] = keys.astype(jnp.bfloat16)
    params, fresh = step(held_ref[0], held_ref[1], pseudo_ref[...])
    params_ref[...] = params
    fresh_ref[...] = fresh


def own_half(core, weight, cotangent, tokens, gain, held, pseudo):
    count, width = tokens.shape
    half = weight.shape[-1]
    vmem = pl.BlockSpec(memory_space=pltpu.VMEM)
    return pl.pallas_call(
        own_kernel,
        out_shape=(
            jax.ShapeDtypeStruct((count, width), jnp.float32),
            jax.ShapeDtypeStruct((count, width), jnp.bfloat16),
            jax.ShapeDtypeStruct((count, 1), jnp.float32),
            jax.ShapeDtypeStruct((count, half), jnp.bfloat16),
            jax.ShapeDtypeStruct(pseudo.shape, jnp.float32),
            jax.ShapeDtypeStruct(pseudo.shape, jnp.float32),
        ),
        in_specs=[pl.BlockSpec(memory_space=pltpu.SMEM)] + [vmem] * 6,
        out_specs=[vmem] * 6,
        compiler_params=pltpu.CompilerParams(vmem_limit_bytes=24 * 1024 * 1024),
        cost_estimate=pl.CostEstimate(flops=900_000_000, bytes_accessed=12_000_000, transcendentals=0),
    )(core.reshape(1), weight, cotangent, tokens, gain, held, pseudo)


def tail_kernel(core_ref, weight_ref, cot_ref, back_ref, hidden_ref, tokens_ref, inverse_ref, gain_ref, mine_ref, keys_out, grads_out, scaled_ref, keys_ref, grads_ref, sems):
    tokens, width = tokens_ref.shape
    row_count, half = weight_ref.shape[-2:]
    parts = [slice(at, at + CHUNK) for at in range(0, width, CHUNK)]
    core = core_ref[0]
    cotangent = cot_ref[:, columns_of(1 - core, half)]
    keys = jnp.zeros((tokens, half), jnp.float32)
    total = jnp.zeros((tokens, HB), jnp.float32)
    for chunk, columns in enumerate(parts):
        rows = jnp.concatenate([weight_ref[at] for at in pieces_of(chunk, row_count)], axis=0)
        back = back_ref[:, columns] + lax.dot_general(
            cotangent, rows, (((1,), (1,)), ((), ())), preferred_element_type=jnp.float32
        )
        keys = keys + jnp.dot(hidden_ref[:, columns], rows, preferred_element_type=jnp.float32)
        scaled = back * gain_ref[:, columns]
        scaled_ref[:, columns] = scaled
        product = scaled * tokens_ref[:, columns].astype(jnp.float32)
        for at in range(0, CHUNK, HB):
            total = total + product[:, at : at + HB]
    keys_ref[:, columns_of(core, half)] = mine_ref[...]
    keys_ref[:, columns_of(1 - core, half)] = keys.astype(jnp.bfloat16)
    copies = [pltpu.make_async_copy(keys_ref, keys_out, sems.at[len(parts)])]
    copies[0].start()
    inverse = inverse_ref[...]
    centre = inverse * jnp.sum(total, axis=1, keepdims=True) / width
    factor = inverse * inverse * centre
    for chunk, columns in enumerate(parts):
        grads = inverse * scaled_ref[:, columns] - factor * tokens_ref[:, columns].astype(jnp.float32)
        grads_ref[:, columns] = grads.astype(jnp.bfloat16)
        copy = pltpu.make_async_copy(grads_ref.at[:, columns], grads_out.at[:, columns], sems.at[chunk])
        copy.start()
        copies.append(copy)
    for copy in copies:
        copy.wait()


def tail(core, weight, cotangent, back, hidden, tokens, inverse, gain, keys_mine):
    count, width = tokens.shape
    half = keys_mine.shape[1]
    vmem = pl.BlockSpec(memory_space=pltpu.VMEM)
    return pl.pallas_call(
        tail_kernel,
        out_shape=(
            jax.ShapeDtypeStruct((count, 2 * half), jnp.bfloat16),
            jax.ShapeDtypeStruct((count, width), jnp.bfloat16),
        ),
        in_specs=[pl.BlockSpec(memory_space=pltpu.SMEM)] + [vmem] * 8,
        out_specs=[pl.BlockSpec(memory_space=pltpu.HBM)] * 2,
        scratch_shapes=[
            pltpu.VMEM((count, width), jnp.float32),
            pltpu.VMEM((count, 2 * half), jnp.bfloat16),
            pltpu.VMEM((count, width), jnp.bfloat16),
            pltpu.SemaphoreType.DMA((width // CHUNK + 1,)),
        ],
        compiler_params=pltpu.CompilerParams(vmem_limit_bytes=20 * 1024 * 1024),
        cost_estimate=pl.CostEstimate(flops=900_000_000, bytes_accessed=12_000_000, transcendentals=0),
    )(core.reshape(1), weight, cotangent, back, hidden, tokens, inverse, gain, keys_mine)


def place(core, y, z, x):
    return (((y // 4 * 2 + core) * 4 + y % 4) * 16 + z) * 4 + x


def pairs():
    groups = []
    for core in range(2):
        for y in (0, 1, 4, 5):
            for z in range(16):
                for x in range(4):
                    groups.append([place(core, y_at, z, x) for y_at in (y, (y + 2 - 4 * core) % 8)])
    return groups


def cubes():
    groups = []
    for core in range(2):
        for y in range(0, 8, 2):
            for z in range(0, 16, 2):
                for x in range(0, 4, 2):
                    group = []
                    for odd in np.ndindex(2, 2, 2):
                        step = [bit * (1 - 2 * core) for bit in odd]
                        group.append(place(core, (y + step[0]) % 8, (z + step[1]) % 16, (x + step[2]) % 4))
                    groups.append(group)
    return groups


def gather(block, axes, count, groups=None):
    copies = jnp.broadcast_to(block[None], (count,) + block.shape)
    return lax.all_to_all(copies, axes, 0, 0, axis_index_groups=groups, tiled=True)


def body(tokens, gain, key_cotangent, global_params, local_params, momentum, sign_bits):
    all_local = gather(local_params[0], REPLICA, 4)
    row_count, width = global_params.shape
    sign_vec = jnp.broadcast_to((2 * sign_bits - 1).astype(jnp.float32), (row_count, width))
    held = lax.optimization_barrier(jnp.stack([global_params, momentum, sign_vec]))
    weight_part, pseudo = outer_update(all_local, held)

    half = width // 2
    core = lax.axis_index("core")
    mine = jnp.where(core == 0, weight_part[:, :half], weight_part[:, half:])
    got = gather(mine, ("zh", "x1"), 16)
    got = gather(got, AXES, 2, pairs())
    got = gather(got, AXES, 8, cubes())
    got = got.reshape(tuple(SIZES[axis] for axis in PIECE_AXES) + (row_count, half))
    other = lax.ppermute(got, "core", [(0, 1), (1, 0)])

    rows, cotangent = tokens[0], key_cotangent[0]
    own = own_half(core, got, cotangent, rows, gain, held, pseudo)
    back, hidden, inverse, keys_mine, new_params, new_momentum = own
    keys, grads = tail(core, other, cotangent, back, hidden, rows, inverse, gain, keys_mine)
    return (keys[None], grads[None], new_params, new_momentum)


def solution(mesh):
    fine = Mesh(mesh.devices.reshape(tuple(SIZES.values())), tuple(SIZES))
    in_specs = (
        P(REPLICA, FSDP, None),
        P(REPLICA, None),
        P(REPLICA, FSDP, None),
        P(FSDP, None),
        P(REPLICA, FSDP, None),
        P(FSDP, None),
        P(),
    )
    out_specs = (
        P(REPLICA, FSDP, None),
        P(REPLICA, FSDP, None),
        P(FSDP, None),
        P(FSDP, None),
    )
    return jax.shard_map(body, mesh=fine, in_specs=in_specs, out_specs=out_specs, check_vma=False)
```

```python
import math

import jax
import jax.numpy as jnp
import numpy as np
from jax import lax
from jax.experimental import pallas as pl
from jax.experimental.pallas import tpu as pltpu
from jax.sharding import Mesh, PartitionSpec as P

HB = 128


NORM_EPS = 1e-06
OUTER_MU = 0.9
OUTER_LR = 0.7
CLIP_LEVEL = 2.0

REPLICA = ("yh", "core")
FSDP = ("y1", "y0", "zh", "z0", "x1", "x0")
SIZES = {"yh": 2, "core": 2, "y1": 2, "y0": 2, "zh": 8, "z0": 2, "x1": 2, "x0": 2}
AXES = tuple(SIZES)


def signs():
    common = lax.broadcasted_iota(jnp.int32, (HB, HB), 0) & lax.broadcasted_iota(jnp.int32, (HB, HB), 1)
    for shift in (4, 2, 1):
        common = common ^ (common >> shift)
    return (1 - 2 * (common & 1)).astype(jnp.float32).astype(jnp.bfloat16)


def rotate(values, matrix):
    total = None
    rest = values
    for _ in range(3):
        part = rest.astype(jnp.bfloat16)
        rest = rest - part.astype(jnp.float32)
        product = jnp.dot(part, matrix, preferred_element_type=jnp.float32)
        total = product if total is None else total + product
    return total * (1.0 / math.sqrt(HB))


def update_kernel(local_ref, held_ref, weight_ref, pseudo_ref):
    replicas, row_count, width = local_ref.shape
    count = width // HB
    matrix = signs()
    sign_vec = held_ref[2]
    global_rows = held_ref[0]
    pieces = []
    for replica in range(replicas):
        drift = (global_rows - local_ref[replica].astype(jnp.float32)) * sign_vec
        pieces += [drift[:, at * HB : (at + 1) * HB] for at in range(count)]
    rotated = rotate(jnp.concatenate(pieces, axis=0), matrix)
    block_scale = jnp.mean(jnp.abs(rotated), axis=-1, keepdims=True) + NORM_EPS
    terms = jnp.clip(rotated / block_scale, -CLIP_LEVEL, CLIP_LEVEL) * block_scale
    terms = terms.astype(jnp.bfloat16).astype(jnp.float32)
    rows = count * row_count
    summed = terms[:rows]
    for replica in range(1, replicas):
        summed = summed + terms[replica * rows : (replica + 1) * rows]
    restored = rotate(summed / replicas, matrix)
    restored = jnp.concatenate([restored[at * row_count : (at + 1) * row_count] for at in range(count)], axis=1)
    pseudo = restored * sign_vec
    params, _ = step(global_rows, held_ref[1], pseudo)
    pseudo_ref[...] = pseudo
    weight_ref[...] = params.astype(jnp.bfloat16)


def step(global_rows, moment_rows, pseudo):
    fresh_moment = OUTER_MU * moment_rows + pseudo
    fresh_params = global_rows - OUTER_LR * (pseudo + OUTER_MU * fresh_moment)
    return (fresh_params, fresh_moment)


def outer_update(all_local, held):
    row_count, width = held.shape[1:]
    return pl.pallas_call(
        update_kernel,
        out_shape=(
            jax.ShapeDtypeStruct((row_count, width), jnp.bfloat16),
            jax.ShapeDtypeStruct((row_count, width), jnp.float32),
        ),
        in_specs=[pl.BlockSpec(memory_space=pltpu.VMEM)] * 2,
        out_specs=[pl.BlockSpec(memory_space=pltpu.VMEM)] * 2,
        compiler_params=pltpu.CompilerParams(vmem_limit_bytes=4 * 1024 * 1024),
        cost_estimate=pl.CostEstimate(flops=20_000_000, bytes_accessed=250_000, transcendentals=0),
    )(all_local, held)


CHUNK = 512
ROWS = 48
PIECE_AXES = ("y0", "z0", "x0", "y1", "x1", "zh")


def pieces_of(chunk, row_count):
    order = ("y1", "y0", "zh", "z0", "x1", "x0")
    sizes = [SIZES[axis] for axis in order]
    count = CHUNK // row_count
    for piece in range(chunk * count, (chunk + 1) * count):
        at = dict(zip(order, np.unravel_index(piece, sizes)))
        yield tuple(int(at[axis]) for axis in PIECE_AXES)


def columns_of(core, half):
    return pl.ds(pl.multiple_of(core * half, half), half)


def own_kernel(core_ref, weight_ref, cot_ref, tokens_ref, gain_ref, held_ref, pseudo_ref, back_ref, hidden_ref, inverse_ref, keys_ref, params_ref, fresh_ref):
    tokens, width = tokens_ref.shape
    row_count, half = weight_ref.shape[-2:]
    parts = [slice(at, at + CHUNK) for at in range(0, width, CHUNK)]
    total = jnp.zeros((tokens, 1), jnp.float32)
    for columns in parts:
        values = tokens_ref[:, columns].astype(jnp.float32)
        total = total + jnp.sum(values * values, axis=1, keepdims=True)
    inverse = lax.rsqrt(total / width + NORM_EPS)
    inverse_ref[...] = inverse
    cotangent = cot_ref[:, columns_of(core_ref[0], half)]
    keys = jnp.zeros((tokens, half), jnp.float32)
    for chunk, columns in enumerate(parts):
        rows = jnp.concatenate([weight_ref[at] for at in pieces_of(chunk, row_count)], axis=0)
        back_ref[:, columns] = lax.dot_general(
            cotangent, rows, (((1,), (1,)), ((), ())), preferred_element_type=jnp.float32
        )
        hidden = (tokens_ref[:, columns].astype(jnp.float32) * inverse * gain_ref[:, columns]).astype(jnp.bfloat16)
        hidden_ref[:, columns] = hidden
        keys = keys + jnp.dot(hidden, rows, preferred_element_type=jnp.float32)
    keys_ref[...] = keys.astype(jnp.bfloat16)
    params, fresh = step(held_ref[0], held_ref[1], pseudo_ref[...])
    params_ref[...] = params
    fresh_ref[...] = fresh


def own_half(core, weight, cotangent, tokens, gain, held, pseudo):
    count, width = tokens.shape
    half = weight.shape[-1]
    vmem = pl.BlockSpec(memory_space=pltpu.VMEM)
    return pl.pallas_call(
        own_kernel,
        out_shape=(
            jax.ShapeDtypeStruct((count, width), jnp.float32),
            jax.ShapeDtypeStruct((count, width), jnp.bfloat16),
            jax.ShapeDtypeStruct((count, 1), jnp.float32),
            jax.ShapeDtypeStruct((count, half), jnp.bfloat16),
            jax.ShapeDtypeStruct(pseudo.shape, jnp.float32),
            jax.ShapeDtypeStruct(pseudo.shape, jnp.float32),
        ),
        in_specs=[pl.BlockSpec(memory_space=pltpu.SMEM)] + [vmem] * 6,
        out_specs=[vmem] * 6,
        compiler_params=pltpu.CompilerParams(vmem_limit_bytes=24 * 1024 * 1024),
        cost_estimate=pl.CostEstimate(flops=900_000_000, bytes_accessed=12_000_000, transcendentals=0),
    )(core.reshape(1), weight, cotangent, tokens, gain, held, pseudo)


def tail_kernel(core_ref, weight_ref, cot_ref, back_ref, hidden_ref, tokens_ref, inverse_ref, gain_ref, mine_ref, keys_out, grads_out, scaled_ref, keys_ref, grads_ref, sems):
    tokens, width = tokens_ref.shape
    row_count, half = weight_ref.shape[-2:]
    parts = [slice(at, at + CHUNK) for at in range(0, width, CHUNK)]
    core = core_ref[0]
    cotangent = cot_ref[:, columns_of(1 - core, half)]
    keys = jnp.zeros((tokens, half), jnp.float32)
    total = jnp.zeros((tokens, HB), jnp.float32)
    for chunk, columns in enumerate(parts):
        rows = jnp.concatenate([weight_ref[at] for at in pieces_of(chunk, row_count)], axis=0)
        back = back_ref[:, columns] + lax.dot_general(
            cotangent, rows, (((1,), (1,)), ((), ())), preferred_element_type=jnp.float32
        )
        keys = keys + jnp.dot(hidden_ref[:, columns], rows, preferred_element_type=jnp.float32)
        scaled = back * gain_ref[:, columns]
        scaled_ref[:, columns] = scaled
        product = scaled * tokens_ref[:, columns].astype(jnp.float32)
        for at in range(0, CHUNK, HB):
            total = total + product[:, at : at + HB]
    keys_ref[:, columns_of(core, half)] = mine_ref[...]
    keys_ref[:, columns_of(1 - core, half)] = keys.astype(jnp.bfloat16)
    copies = [pltpu.make_async_copy(keys_ref, keys_out, sems.at[tokens // ROWS])]
    copies[0].start()
    inverse = inverse_ref[...]
    centre = inverse * jnp.sum(total, axis=1, keepdims=True) / width
    factor = inverse * inverse * centre
    for step_at, first in enumerate(range(0, tokens, ROWS)):
        block = slice(first, first + ROWS)
        for columns in parts:
            values = tokens_ref[block, columns].astype(jnp.float32)
            grads = inverse[block] * scaled_ref[block, columns] - factor[block] * values
            grads_ref[block, columns] = grads.astype(jnp.bfloat16)
        copy = pltpu.make_async_copy(grads_ref.at[block, :], grads_out.at[block, :], sems.at[step_at])
        copy.start()
        copies.append(copy)
    for copy in copies:
        copy.wait()


def tail(core, weight, cotangent, back, hidden, tokens, inverse, gain, keys_mine):
    count, width = tokens.shape
    half = keys_mine.shape[1]
    vmem = pl.BlockSpec(memory_space=pltpu.VMEM)
    return pl.pallas_call(
        tail_kernel,
        out_shape=(
            jax.ShapeDtypeStruct((count, 2 * half), jnp.bfloat16),
            jax.ShapeDtypeStruct((count, width), jnp.bfloat16),
        ),
        in_specs=[pl.BlockSpec(memory_space=pltpu.SMEM)] + [vmem] * 8,
        out_specs=[pl.BlockSpec(memory_space=pltpu.HBM)] * 2,
        scratch_shapes=[
            pltpu.VMEM((count, width), jnp.float32),
            pltpu.VMEM((count, 2 * half), jnp.bfloat16),
            pltpu.VMEM((count, width), jnp.bfloat16),
            pltpu.SemaphoreType.DMA((count // ROWS + 1,)),
        ],
        compiler_params=pltpu.CompilerParams(vmem_limit_bytes=20 * 1024 * 1024),
        cost_estimate=pl.CostEstimate(flops=900_000_000, bytes_accessed=12_000_000, transcendentals=0),
    )(core.reshape(1), weight, cotangent, back, hidden, tokens, inverse, gain, keys_mine)


def place(core, y, z, x):
    return (((y // 4 * 2 + core) * 4 + y % 4) * 16 + z) * 4 + x


def cubes():
    groups = []
    for core in range(2):
        for y in range(0, 8, 2):
            for z in range(0, 16, 2):
                for x in range(0, 4, 2):
                    group = []
                    for odd in np.ndindex(2, 2, 2):
                        step = [bit * (1 - 2 * core) for bit in odd]
                        group.append(place(core, (y + step[0]) % 8, (z + step[1]) % 16, (x + step[2]) % 4))
                    groups.append(group)
    return groups


def gather(block, axes, count, groups=None):
    copies = jnp.broadcast_to(block[None], (count,) + block.shape)
    return lax.all_to_all(copies, axes, 0, 0, axis_index_groups=groups, tiled=True)


def body(tokens, gain, key_cotangent, global_params, local_params, momentum, sign_bits):
    all_local = gather(local_params[0], REPLICA, 4)
    row_count, width = global_params.shape
    sign_vec = jnp.broadcast_to((2 * sign_bits - 1).astype(jnp.float32), (row_count, width))
    held = lax.optimization_barrier(jnp.stack([global_params, momentum, sign_vec]))
    weight_part, pseudo = outer_update(all_local, held)

    half = width // 2
    core = lax.axis_index("core")
    mine = jnp.where(core == 0, weight_part[:, :half], weight_part[:, half:])
    got = gather(mine, ("zh",), 8)
    got = gather(got, ("y1", "x1"), 4)
    got = gather(got, AXES, 8, cubes())
    got = got.reshape(tuple(SIZES[axis] for axis in PIECE_AXES) + (row_count, half))
    other = lax.ppermute(got, "core", [(0, 1), (1, 0)])

    rows, cotangent = tokens[0], key_cotangent[0]
    own = own_half(core, got, cotangent, rows, gain, held, pseudo)
    back, hidden, inverse, keys_mine, new_params, new_momentum = own
    keys, grads = tail(core, other, cotangent, back, hidden, rows, inverse, gain, keys_mine)
    return (keys[None], grads[None], new_params, new_momentum)


def solution(mesh):
    fine = Mesh(mesh.devices.reshape(tuple(SIZES.values())), tuple(SIZES))
    in_specs = (
        P(REPLICA, FSDP, None),
        P(REPLICA, None),
        P(REPLICA, FSDP, None),
        P(FSDP, None),
        P(REPLICA, FSDP, None),
        P(FSDP, None),
        P(),
    )
    out_specs = (
        P(REPLICA, FSDP, None),
        P(REPLICA, FSDP, None),
        P(FSDP, None),
        P(FSDP, None),
    )
    return jax.shard_map(body, mesh=fine, in_specs=in_specs, out_specs=out_specs, check_vma=False)
```
